32 devices in a mesh: pair: 8 (over z, x), vgrp: 4 (over y, core).
Axes of the slice: x: 2, y: 2, z: 4, core: 2. Of those that a mesh axis runs over, the one named last changes fastest.
Arguments:
- amplitudes: bfloat16 [16, 768, 768], P('pair'), may hold values from -6 to 6
- cholesky_vectors: bfloat16 [4, 8, 768, 768], P('vgrp', 'pair'), may hold values from -0.21875 to 0.21875
- owner_order: int32 [4, 4], replicated, may hold values from 0 to 7, as said below
Outputs:
- residual: float32 [16, 768, 768], P('pair', 'vgrp')
The draws below stay inside these ranges and needn't reach their ends.
Inputs may be any that keep to these rules, and one draw needn't show every extreme that they name: `owner_order`: within one row the 4 entries are distinct; in every draw some row names both 0 and 7.
All inputs are finite; a program needn't handle non-finite values.
Results may differ from the reference program's by a relative error of at most 0.0029.
Values may be sent and summed in bfloat16 or wider, within the bound.
A program may use at most 64 MiB of HBM per device.

```python
import jax
import jax.numpy as jnp
from jax import lax

V = 768
VECS = 4
PAIRS = 16
OWNERS = 8
GROUPS = 4


def draw_owner_order(key, part):
    keyring = jax.random.split(key, GROUPS + 1)
    chosen = jax.random.randint(keyring[0], (), 0, GROUPS)

    def one_group(subkey):
        key_drawn, key_inner, key_order = jax.random.split(subkey, 3)
        drawn = jax.random.permutation(key_drawn, OWNERS)[:VECS].astype(jnp.int32)
        inner = (jax.random.permutation(key_inner, OWNERS - 2)[:VECS - 2] + 1).astype(jnp.int32)
        ends = jnp.concatenate([jnp.array([0, OWNERS - 1], jnp.int32), inner])
        ends = ends[jax.random.permutation(key_order, VECS)]
        return (drawn, ends)
    plains, endings = jax.vmap(one_group)(keyring[1:])
    group_ids = jnp.arange(GROUPS, dtype=jnp.int32)[:, None]
    return jnp.where(group_ids == chosen, endings, plains).astype(jnp.int32)


def levels(key, extent, pieces, least, largest):
    loudness, own = 1.0, jax.random.fold_in(key, 6)
    for axis_at, blocks in pieces:
        draws = jnp.exp(jax.random.uniform(jax.random.fold_in(own, axis_at), (blocks,), jnp.float32, least / len(pieces), largest / len(pieces)))
        loudness = loudness * jnp.repeat(draws, extent[axis_at] // blocks).reshape([-1 if axis == axis_at else 1 for axis in range(len(extent))])
    return loudness


def noise(key, extent, deviation, limit, cuts=(), kind=jnp.bfloat16):
    result = deviation * jax.random.normal(key, extent, jnp.float32)
    if cuts:
        result = result * levels(key, extent, cuts, -0.22, 0.18)
    return jnp.clip(result, -limit, limit).astype(kind)


def setup_inputs(seed: int = 0) -> dict:
    keys = jax.random.split(jax.random.key(seed), 4)
    amplitudes = noise(keys[0], (PAIRS, V, V), 1.0, 6.0, ((0, 8),))
    cholesky_vectors = noise(keys[1], (GROUPS, OWNERS, V, V), V ** -0.5, 0.21875, ((0, 4), (1, 8)))
    owner_order = draw_owner_order(jax.random.fold_in(keys[3], 71), 0)
    return {"amplitudes": amplitudes, "cholesky_vectors": cholesky_vectors, "owner_order": owner_order}


def reference(amplitudes, cholesky_vectors, owner_order):
    group_rows = jnp.arange(GROUPS, dtype=jnp.int32)[:, None]
    selected = cholesky_vectors[group_rows, owner_order].reshape(GROUPS * VECS, V, V)

    def one_pair(amplitude):
        def add_vector(accumulated, vector):
            half_product = jnp.dot(vector, amplitude, preferred_element_type=jnp.float32).astype(jnp.bfloat16)
            return accumulated + jnp.dot(half_product, vector.T, preferred_element_type=jnp.float32), None

        accumulated, unused = lax.scan(add_vector, jnp.zeros((V, V), jnp.float32), selected)
        return accumulated

    return lax.map(one_pair, amplitudes)
```

```python
import functools

import jax
import jax.numpy as jnp
from jax import lax
from jax.experimental import pallas as pl
from jax.experimental.pallas import tpu as pltpu
from jax.sharding import PartitionSpec as P

MESH = pl.DeviceIdType.MESH
CHUNKS = 4
LAG = 2
F32 = jnp.float32
BF16 = jnp.bfloat16


def kernel(
    nz, slots, owner_ref, amp_hbm, vec_ref, out_ref,
    amp, near, right_in, left_in, right_out, left_out, vectors, halves, acc,
    core_out, core_in, y_out, y_in,
    amp_sem, near_send, near_recv, rs_sem, rr_sem, ls_sem, lr_sem,
    fs_sem, fr_sem, cs_sem, cr_sem, ys_sem, yr_sem,
):
    pair = lax.axis_index("pair")
    grp = lax.axis_index("vgrp")
    z, x = pair // 2, pair % 2
    y, core = grp // 2, grp % 2
    size = vec_ref.shape[0]
    half = size // 2
    part = half // CHUNKS
    items = slots * CHUNKS
    pairs, tile = out_ref.shape[0], out_ref.shape[1]
    last = nz - 1

    x_dev = {"pair": z * 2 + (1 - x), "vgrp": grp}
    up_dev = {"pair": ((z + 1) % nz) * 2 + x, "vgrp": grp}
    down_dev = {"pair": ((z + last) % nz) * 2 + x, "vgrp": grp}
    core_dev = {"pair": pair, "vgrp": y * 2 + (1 - core)}
    y_dev = {"pair": pair, "vgrp": (1 - y) * 2 + core}

    load = pltpu.make_async_copy(amp_hbm, amp, amp_sem)
    load.start()

    barrier = pltpu.get_barrier_semaphore()
    for dev in (x_dev, up_dev, down_dev, core_dev, y_dev):
        pl.semaphore_signal(barrier, inc=1, device_id=dev, device_id_type=MESH)
    pl.semaphore_wait(barrier, 5)

    def remote(src, dst, send, recv, dev):
        return pltpu.make_async_remote_copy(
            src_ref=src, dst_ref=dst, send_sem=send, recv_sem=recv,
            device_id=dev, device_id_type=MESH,
        )

    def near_copy(c):
        rows = pl.ds(pl.multiple_of((1 - x) * half + c * part, 16), part)
        return remote(vec_ref.at[rows], near.at[c], near_send.at[c], near_recv.at[c], x_dev)

    def right_copy(i):
        return remote(right_out.at[i], right_in.at[i], rs_sem.at[i], rr_sem.at[i], up_dev)

    def left_copy(i):
        return remote(left_out.at[i], left_in.at[i], ls_sem.at[i], lr_sem.at[i], down_dev)

    def my_rows(i):
        return pl.ds(pl.multiple_of(x * half + (i % CHUNKS) * part, 16), part)

    def final_copy(i):
        view = vectors.at[i // CHUNKS, my_rows(i)]
        return remote(view, view, fs_sem.at[i], fr_sem.at[i], x_dev)

    def owner(i):
        o = owner_ref[grp, i // CHUNKS]
        return o // 2, o % 2

    def local(i):
        unused, ox = owner(i)
        return lax.select(ox == x, vec_ref[my_rows(i), :], near[i % CHUNKS])

    for c in range(CHUNKS):
        near_copy(c).start()
    acc[...] = jnp.zeros_like(acc)

    lag_r = LAG * z
    lag_l = LAG * (last - z)
    lag_f = LAG * last
    first = lag_f + CHUNKS + 1
    per_slot = 2 * pairs + 4

    def through(k, rows):
        lhs = halves[:, rows, :].reshape(pairs * tile, size)
        more = lax.dot_general(
            lhs, vectors[k], (((1,), (1,)), ((), ())), preferred_element_type=F32
        ).reshape(pairs, tile, size)
        return acc[:, rows, :] + more

    def piece(q):
        k, j = q // per_slot, q % per_slot

        @pl.when(j == 0)
        def _():
            for c in range(CHUNKS):
                final_copy(k * CHUNKS + c).wait_recv()

        @pl.when(j < 2 * pairs)
        def _():
            p = j // 2
            rows = pl.ds(pl.multiple_of((j % 2) * half, 16), half)
            halves[p, rows, :] = jnp.dot(
                vectors[k, rows, :], amp[p], preferred_element_type=F32
            ).astype(BF16)

        @pl.when(j >= 2 * pairs)
        def _():
            rows = pl.ds(pl.multiple_of((j - 2 * pairs) * tile, 16), tile)
            acc[:, rows, :] = through(k, rows)

    def step(t, carry):
        @pl.when(t < CHUNKS)
        def _():
            near_copy(t).wait_recv()

        i = t - lag_r

        @pl.when((i >= 0) & (i < items))
        def _():
            @pl.when(z > 0)
            def _():
                right_copy(i).wait_recv()

            @pl.when(z == 0)
            def _():
                right_out[i] = local(i)
                right_copy(i).start()

            @pl.when((z > 0) & (z < last))
            def _():
                oz, unused = owner(i)
                right_out[i] = lax.select(oz == z, local(i), right_in[i])
                right_copy(i).start()

        j = t - lag_l

        @pl.when((j >= 0) & (j < items))
        def _():
            @pl.when(z < last)
            def _():
                left_copy(j).wait_recv()

            @pl.when(z == last)
            def _():
                left_out[j] = local(j)
                left_copy(j).start()

            @pl.when((z > 0) & (z < last))
            def _():
                oz, unused = owner(j)
                left_out[j] = lax.select(oz == z, local(j), left_in[j])
                left_copy(j).start()

        f = t - lag_f

        @pl.when((f >= 0) & (f < items))
        def _():
            oz, unused = owner(f)
            k, rows = f // CHUNKS, my_rows(f)

            @pl.when(z == 0)
            def _():
                vectors[k, rows, :] = lax.select(oz == z, local(f), left_in[f])

            @pl.when(z == last)
            def _():
                vectors[k, rows, :] = lax.select(oz == z, local(f), right_in[f])

            @pl.when((z > 0) & (z < last))
            def _():
                came = lax.select(oz < z, right_in[f], left_in[f])
                vectors[k, rows, :] = lax.select(oz == z, local(f), came)

            final_copy(f).start()

        @pl.when(t == first)
        def _():
            load.wait()

        q = (t - first) * 2
        for n in range(2):
            @pl.when((q + n >= 0) & (q + n < slots * per_slot - 4))
            def _():
                piece(q + n)

        return carry

    lax.fori_loop(0, first + slots * per_slot // 2, step, 0)

    k = slots - 1

    def rows_of(yy, cc):
        return pl.ds(pl.multiple_of((yy * 2 + cc) * tile, 16), tile)

    def core_copy(n):
        return remote(core_out.at[n], core_in.at[n], cs_sem.at[n], cr_sem.at[n], core_dev)

    def y_copy(p):
        return remote(y_out.at[p], y_in.at[p], ys_sem.at[p], yr_sem.at[p], y_dev)

    core_out[0] = through(k, rows_of(1 - y, 1 - core)).astype(BF16)
    core_copy(0).start()
    core_out[1] = through(k, rows_of(y, 1 - core)).astype(BF16)
    core_copy(1).start()
    rows = rows_of(1 - y, core)
    acc[:, rows, :] = through(k, rows)
    core_copy(0).wait_recv()
    for p in range(pairs):
        y_out[p] = (acc[p, rows, :] + core_in[0, p].astype(F32)).astype(BF16)
        y_copy(p).start()
    rows = rows_of(y, core)
    acc[:, rows, :] = through(k, rows)
    core_copy(1).wait_recv()
    for p in range(pairs):
        y_copy(p).wait_recv()
        out_ref[p] = acc[p, rows, :] + core_in[1, p].astype(F32) + y_in[p].astype(F32)

    for c in range(CHUNKS):
        near_copy(c).wait_send()

    def drain(i, carry):
        @pl.when(z < last)
        def _():
            right_copy(i).wait_send()

        @pl.when(z > 0)
        def _():
            left_copy(i).wait_send()

        final_copy(i).wait_send()
        return carry

    lax.fori_loop(0, items, drain, 0)
    for n in range(2):
        core_copy(n).wait_send()
    for p in range(pairs):
        y_copy(p).wait_send()


def on_device(pair_size, amplitudes, cholesky_vectors, owner_order):
    pairs, size, unused = amplitudes.shape
    slots = owner_order.shape[1]
    half = size // 2
    part = half // CHUNKS
    items = slots * CHUNKS
    tile = size // 4
    dma = pltpu.SemaphoreType.DMA
    vmem = pltpu.VMEM
    return pl.pallas_call(
        functools.partial(kernel, pair_size // 2, slots),
        out_shape=jax.ShapeDtypeStruct((pairs, tile, size), F32),
        in_specs=[
            pl.BlockSpec(memory_space=pltpu.SMEM),
            pl.BlockSpec(memory_space=pl.ANY),
            pl.BlockSpec(memory_space=pltpu.VMEM),
        ],
        out_specs=pl.BlockSpec(memory_space=pltpu.VMEM),
        scratch_shapes=[
            vmem((pairs, size, size), BF16),
            vmem((CHUNKS, part, size), BF16),
            vmem((items, part, size), BF16),
            vmem((items, part, size), BF16),
            vmem((items, part, size), BF16),
            vmem((items, part, size), BF16),
            vmem((slots, size, size), BF16),
            vmem((pairs, size, size), BF16),
            vmem((pairs, size, size), F32),
            vmem((2, pairs, tile, size), BF16),
            vmem((2, pairs, tile, size), BF16),
            vmem((pairs, tile, size), BF16),
            vmem((pairs, tile, size), BF16),
            dma,
            dma((CHUNKS,)), dma((CHUNKS,)),
            dma((items,)), dma((items,)),
            dma((items,)), dma((items,)),
            dma((items,)), dma((items,)),
            dma((2,)), dma((2,)),
            dma((pairs,)), dma((pairs,)),
        ],
        compiler_params=pltpu.CompilerParams(
            collective_id=0, has_side_effects=True, vmem_limit_bytes=52 * 2 ** 20
        ),
        cost_estimate=pl.CostEstimate(
            flops=4 * pairs * slots * size ** 3, bytes_accessed=8 * pairs * size ** 2,
            transcendentals=0,
        ),
    )(owner_order, amplitudes, cholesky_vectors[0, 0])


def solution(mesh):
    placed = (P("pair", None, None), P("vgrp", "pair", None, None), P())
    return jax.shard_map(
        functools.partial(on_device, mesh.shape["pair"]), mesh=mesh, in_specs=placed,
        out_specs=P("pair", "vgrp", None), check_vma=False,
    )
```

```python
import functools

import jax
import jax.numpy as jnp
from jax import lax
from jax.experimental import pallas as pl
from jax.experimental.pallas import tpu as pltpu
from jax.sharding import PartitionSpec as P

MESH = pl.DeviceIdType.MESH
COLS = 128
LAG = 2
F32 = jnp.float32
BF16 = jnp.bfloat16


def kernel(
    nz, slots, owner_ref, amp_hbm, vec_ref, out_ref,
    amp, near, right_in, left_in, right_out, left_out, vectors, turned, halves, acc,
    core_out, core_in, keep, y_out, y_in, rest_out, rest_in,
    amp_sem, near_send, near_recv, rs_sem, rr_sem, ls_sem, lr_sem,
    fs_sem, fr_sem, cs_sem, cr_sem, ys_sem, yr_sem, es_sem, er_sem,
):
    pair = lax.axis_index("pair")
    grp = lax.axis_index("vgrp")
    z, x = pair // 2, pair % 2
    y, core = grp // 2, grp % 2
    size = vec_ref.shape[0]
    half = size // 2
    part = COLS // 2
    chunks = size // COLS
    early = chunks // 2
    items = slots * chunks
    pairs, tile = out_ref.shape[0], out_ref.shape[1]
    last = nz - 1

    x_dev = {"pair": z * 2 + (1 - x), "vgrp": grp}
    up_dev = {"pair": ((z + 1) % nz) * 2 + x, "vgrp": grp}
    down_dev = {"pair": ((z + last) % nz) * 2 + x, "vgrp": grp}
    core_dev = {"pair": pair, "vgrp": y * 2 + (1 - core)}
    y_dev = {"pair": pair, "vgrp": (1 - y) * 2 + core}

    load = pltpu.make_async_copy(amp_hbm, amp, amp_sem)
    load.start()

    barrier = pltpu.get_barrier_semaphore()
    for dev in (x_dev, up_dev, down_dev, core_dev, y_dev):
        pl.semaphore_signal(barrier, inc=1, device_id=dev, device_id_type=MESH)
    pl.semaphore_wait(barrier, 5)

    def remote(src, dst, send, recv, dev):
        return pltpu.make_async_remote_copy(
            src_ref=src, dst_ref=dst, send_sem=send, recv_sem=recv,
            device_id=dev, device_id_type=MESH,
        )

    def start_of(c):
        there = (c // early) * y + (1 - c // early) * (1 - y)
        return there * half + (c % early) * COLS

    def rows_at(c, xx):
        return pl.ds(pl.multiple_of(start_of(c) + xx * part, 16), part)

    def block_at(c):
        return pl.ds(pl.multiple_of(start_of(c), COLS), COLS)

    def near_copy(c):
        return remote(
            vec_ref.at[rows_at(c, 1 - x)], near.at[c], near_send.at[c], near_recv.at[c], x_dev
        )

    def right_copy(i):
        return remote(right_out.at[i], right_in.at[i], rs_sem.at[i], rr_sem.at[i], up_dev)

    def left_copy(i):
        return remote(left_out.at[i], left_in.at[i], ls_sem.at[i], lr_sem.at[i], down_dev)

    def my_rows(i):
        return rows_at(i // slots, x)

    def final_copy(i):
        view = vectors.at[i % slots, my_rows(i)]
        return remote(view, view, fs_sem.at[i], fr_sem.at[i], x_dev)

    def owner(i):
        o = owner_ref[grp, i % slots]
        return o // 2, o % 2

    def local(i):
        unused, ox = owner(i)
        return lax.select(ox == x, vec_ref[my_rows(i), :], near[i // slots])

    def core_copy(d):
        return remote(core_out.at[d], core_in.at[d], cs_sem.at[d], cr_sem.at[d], core_dev)

    def y_copy(d):
        return remote(y_out.at[d], y_in.at[d], ys_sem.at[d], yr_sem.at[d], y_dev)

    rest_copy = remote(rest_out, rest_in, es_sem, er_sem, core_dev)

    for c in range(chunks):
        near_copy(c).start()

    lag_r = LAG * z
    lag_l = LAG * (last - z)
    lag_f = LAG * last
    first = lag_f + slots + 1

    def block(rows, count, cols):
        total = None
        for k in range(slots):
            term = jnp.dot(
                halves[:, k, rows, :].reshape(pairs * count, size), turned[k, :, cols],
                preferred_element_type=F32,
            )
            total = term if total is None else total + term
        return total.reshape(pairs, count, -1)

    def tile_at(yy, cc):
        return pl.ds(pl.multiple_of((yy * 2 + cc) * tile, 16), tile)

    def early_block(d):
        cols = block_at(d)
        core_out[d] = block(tile_at(1 - y, 1 - core), tile, cols).astype(BF16)
        core_copy(d).start()
        keep[d] = block(tile_at(1 - y, core), tile, cols)

    def early_send(d):
        core_copy(d).wait_recv()
        y_out[d] = (keep[d] + core_in[d].astype(F32)).astype(BF16)
        y_copy(d).start()

    others = pl.ds(pl.multiple_of((1 - y) * half, COLS), half)
    mine = pl.ds(pl.multiple_of(y * half, COLS), half)

    def half_of(c, p):
        rows = block_at(c)
        lhs = vectors[:, rows, :].reshape(slots * COLS, size)
        halves[p, :, rows, :] = (
            jnp.dot(lhs, amp[p], preferred_element_type=F32)
            .astype(BF16).reshape(slots, COLS, size)
        )

    def piece(c, r):
        @pl.when(r == 0)
        def _():
            for k in range(slots):
                final_copy(c * slots + k).wait_recv()
            for k in range(slots):
                turned[k, :, block_at(c)] = vectors[k, block_at(c), :].T
            half_of(c, 0)

        @pl.when(r == 1)
        def _():
            for p in range(1, pairs):
                half_of(c, p)

        @pl.when((r == 2) & (c == early - 1))
        def _():
            for d in range(early):
                early_block(d)

        @pl.when((r == 2) & (c >= early))
        def _():
            early_block(c)

        @pl.when((r == 3) & (c == early - 1))
        def _():
            for d in range(early):
                early_send(d)

        @pl.when((r == 3) & (c >= early))
        def _():
            at = pl.ds(pl.multiple_of((c - early) * COLS, 16), COLS)
            acc[:, at, others] = block(block_at(c), COLS, others)
            early_send(c)

    def step(t, carry):
        @pl.when((t < items) & (t % slots == 0))
        def _():
            near_copy(t // slots).wait_recv()

        i = t - lag_r

        @pl.when((i >= 0) & (i < items))
        def _():
            @pl.when(z > 0)
            def _():
                right_copy(i).wait_recv()

            @pl.when(z == 0)
            def _():
                right_out[i] = local(i)
                right_copy(i).start()

            @pl.when((z > 0) & (z < last))
            def _():
                oz, unused = owner(i)
                right_out[i] = lax.select(oz == z, local(i), right_in[i])
                right_copy(i).start()

        j = t - lag_l

        @pl.when((j >= 0) & (j < items))
        def _():
            @pl.when(z < last)
            def _():
                left_copy(j).wait_recv()

            @pl.when(z == last)
            def _():
                left_out[j] = local(j)
                left_copy(j).start()

            @pl.when((z > 0) & (z < last))
            def _():
                oz, unused = owner(j)
                left_out[j] = lax.select(oz == z, local(j), left_in[j])
                left_copy(j).start()

        f = t - lag_f

        @pl.when((f >= 0) & (f < items))
        def _():
            oz, unused = owner(f)
            k, rows = f % slots, my_rows(f)

            @pl.when(z == 0)
            def _():
                vectors[k, rows, :] = lax.select(oz == z, local(f), left_in[f])

            @pl.when(z == last)
            def _():
                vectors[k, rows, :] = lax.select(oz == z, local(f), right_in[f])

            @pl.when((z > 0) & (z < last))
            def _():
                came = lax.select(oz < z, right_in[f], left_in[f])
                vectors[k, rows, :] = lax.select(oz == z, local(f), came)

            final_copy(f).start()

        @pl.when(t == first)
        def _():
            load.wait()

        @pl.when(t >= first)
        def _():
            piece((t - first) // 4, (t - first) % 4)

        return carry

    lax.fori_loop(0, first + chunks * 4, step, 0)

    def sub(cc):
        return pl.ds(pl.multiple_of(cc * tile, 16), tile)

    rest_out[:, :, mine] = block(tile_at(y, 1 - core), tile, mine).astype(BF16)
    rest_out[:, :, others] = acc[:, sub(1 - core), others].astype(BF16)
    rest_copy.start()
    acc[:, sub(core), mine] = block(tile_at(y, core), tile, mine)
    rest_copy.wait_recv()
    for d in range(chunks):
        cols = block_at((d + early) % chunks)
        y_copy(d).wait_recv()
        out_ref[:, :, cols] = (
            acc[:, sub(core), cols] + rest_in[:, :, cols].astype(F32) + y_in[d].astype(F32)
        )

    for c in range(chunks):
        near_copy(c).wait_send()
        core_copy(c).wait_send()
        y_copy(c).wait_send()
    rest_copy.wait_send()

    def drain(i, carry):
        @pl.when(z < last)
        def _():
            right_copy(i).wait_send()

        @pl.when(z > 0)
        def _():
            left_copy(i).wait_send()

        final_copy(i).wait_send()
        return carry

    lax.fori_loop(0, items, drain, 0)


def on_device(pair_size, amplitudes, cholesky_vectors, owner_order):
    pairs, size, unused = amplitudes.shape
    slots = owner_order.shape[1]
    part = COLS // 2
    chunks = size // COLS
    items = slots * chunks
    tile = size // 4
    dma = pltpu.SemaphoreType.DMA
    vmem = pltpu.VMEM
    return pl.pallas_call(
        functools.partial(kernel, pair_size // 2, slots),
        out_shape=jax.ShapeDtypeStruct((pairs, tile, size), F32),
        in_specs=[
            pl.BlockSpec(memory_space=pltpu.SMEM),
            pl.BlockSpec(memory_space=pl.ANY),
            pl.BlockSpec(memory_space=pltpu.VMEM),
        ],
        out_specs=pl.BlockSpec(memory_space=pltpu.VMEM),
        scratch_shapes=[
            vmem((pairs, size, size), BF16),
            vmem((chunks, part, size), BF16),
            vmem((items, part, size), BF16),
            vmem((items, part, size), BF16),
            vmem((items, part, size), BF16),
            vmem((items, part, size), BF16),
            vmem((slots, size, size), BF16),
            vmem((slots, size, size), BF16),
            vmem((pairs, slots, size, size), BF16),
            vmem((pairs, size // 2, size), F32),
            vmem((chunks, pairs, tile, COLS), BF16),
            vmem((chunks, pairs, tile, COLS), BF16),
            vmem((chunks, pairs, tile, COLS), F32),
            vmem((chunks, pairs, tile, COLS), BF16),
            vmem((chunks, pairs, tile, COLS), BF16),
            vmem((pairs, tile, size), BF16),
            vmem((pairs, tile, size), BF16),
            dma,
            dma((chunks,)), dma((chunks,)),
            dma((items,)), dma((items,)),
            dma((items,)), dma((items,)),
            dma((items,)), dma((items,)),
            dma((chunks,)), dma((chunks,)),
            dma((chunks,)), dma((chunks,)),
            dma, dma,
        ],
        compiler_params=pltpu.CompilerParams(
            collective_id=0, has_side_effects=True, vmem_limit_bytes=58 * 2 ** 20
        ),
        cost_estimate=pl.CostEstimate(
            flops=4 * pairs * slots * size ** 3, bytes_accessed=8 * pairs * size ** 2,
            transcendentals=0,
        ),
    )(owner_order, amplitudes, cholesky_vectors[0, 0])


def solution(mesh):
    placed = (P("pair", None, None), P("vgrp", "pair", None, None), P())
    return jax.shard_map(
        functools.partial(on_device, mesh.shape["pair"]), mesh=mesh, in_specs=placed,
        out_specs=P("pair", "vgrp", None), check_vma=False,
    )
```

```python
import functools

import jax
import jax.numpy as jnp
from jax import lax
from jax.experimental import pallas as pl
from jax.experimental.pallas import tpu as pltpu
from jax.sharding import PartitionSpec as P

MESH = pl.DeviceIdType.MESH
COLS = 128
SPLIT = 2
LAG = 3
F32 = jnp.float32
BF16 = jnp.bfloat16


def kernel(
    nz, slots, owner_ref, amp_hbm, vec_ref, out_ref,
    amp, near, right_in, left_in, right_out, left_out, vectors, turned, halves, acc,
    core_out, core_in, keep, y_out, y_in, rest_out, rest_in,
    amp_sem, near_send, near_recv, rs_sem, rr_sem, ls_sem, lr_sem,
    fs_sem, fr_sem, cs_sem, cr_sem, ys_sem, yr_sem, es_sem, er_sem,
):
    pair = lax.axis_index("pair")
    grp = lax.axis_index("vgrp")
    z, x = pair // 2, pair % 2
    y, core = grp // 2, grp % 2
    size = vec_ref.shape[0]
    half = size // 2
    part = COLS // 2 // SPLIT
    chunks = size // COLS
    early = chunks // 2
    steps = slots * SPLIT
    items = steps * chunks
    pairs, tile = out_ref.shape[0], out_ref.shape[1]
    last = nz - 1

    x_dev = {"pair": z * 2 + (1 - x), "vgrp": grp}
    up_dev = {"pair": ((z + 1) % nz) * 2 + x, "vgrp": grp}
    down_dev = {"pair": ((z + last) % nz) * 2 + x, "vgrp": grp}
    core_dev = {"pair": pair, "vgrp": y * 2 + (1 - core)}
    y_dev = {"pair": pair, "vgrp": (1 - y) * 2 + core}

    load = pltpu.make_async_copy(amp_hbm, amp, amp_sem)
    load.start()

    barrier = pltpu.get_barrier_semaphore()
    for dev in (x_dev, up_dev, down_dev, core_dev, y_dev):
        pl.semaphore_signal(barrier, inc=1, device_id=dev, device_id_type=MESH)
    pl.semaphore_wait(barrier, 5)

    def remote(src, dst, send, recv, dev):
        return pltpu.make_async_remote_copy(
            src_ref=src, dst_ref=dst, send_sem=send, recv_sem=recv,
            device_id=dev, device_id_type=MESH,
        )

    def start_of(c):
        there = (c // early) * y + (1 - c // early) * (1 - y)
        return there * half + (c % early) * COLS

    def rows_at(n, xx):
        at = start_of(n // SPLIT) + (xx * SPLIT + n % SPLIT) * part
        return pl.ds(pl.multiple_of(at, 16), part)

    def block_at(c):
        return pl.ds(pl.multiple_of(start_of(c), COLS), COLS)

    def near_copy(c):
        return remote(
            vec_ref.at[rows_at(c, 1 - x)], near.at[c], near_send.at[c], near_recv.at[c], x_dev
        )

    def right_copy(i):
        return remote(right_out.at[i], right_in.at[i], rs_sem.at[i], rr_sem.at[i], up_dev)

    def left_copy(i):
        return remote(left_out.at[i], left_in.at[i], ls_sem.at[i], lr_sem.at[i], down_dev)

    def my_rows(i):
        return rows_at(i // slots, x)

    def final_copy(i):
        view = vectors.at[i % slots, my_rows(i)]
        return remote(view, view, fs_sem.at[i], fr_sem.at[i], x_dev)

    def owner(i):
        o = owner_ref[grp, i % slots]
        return o // 2, o % 2

    def local(i):
        unused, ox = owner(i)
        return lax.select(ox == x, vec_ref[my_rows(i), :], near[i // slots])

    def core_copy(d):
        return remote(core_out.at[d], core_in.at[d], cs_sem.at[d], cr_sem.at[d], core_dev)

    def y_copy(d):
        return remote(y_out.at[d], y_in.at[d], ys_sem.at[d], yr_sem.at[d], y_dev)

    rest_copy = remote(rest_out, rest_in, es_sem, er_sem, core_dev)

    for c in range(chunks * SPLIT):
        near_copy(c).start()

    lag_r = LAG * z
    lag_l = LAG * (last - z)
    lag_f = LAG * last
    first = lag_f + steps + 1

    def block(rows, count, cols):
        total = None
        for k in range(slots):
            term = jnp.dot(
                halves[:, k, rows, :].reshape(pairs * count, size), turned[k, :, cols],
                preferred_element_type=F32,
            )
            total = term if total is None else total + term
        return total.reshape(pairs, count, -1)

    def tile_at(yy, cc):
        return pl.ds(pl.multiple_of((yy * 2 + cc) * tile, 16), tile)

    def early_block(d):
        cols = block_at(d)
        core_out[d] = block(tile_at(1 - y, 1 - core), tile, cols).astype(BF16)
        core_copy(d).start()
        keep[d] = block(tile_at(1 - y, core), tile, cols)

    def early_send(d):
        core_copy(d).wait_recv()
        y_out[d] = (keep[d] + core_in[d].astype(F32)).astype(BF16)
        y_copy(d).start()

    others = pl.ds(pl.multiple_of((1 - y) * half, COLS), half)
    mine = pl.ds(pl.multiple_of(y * half, COLS), half)

    def half_of(c, p, k0):
        rows = block_at(c)
        count = slots // 2
        lhs = vectors[pl.ds(k0, count), rows, :].reshape(count * COLS, size)
        halves[p, pl.ds(k0, count), rows, :] = (
            jnp.dot(lhs, amp[p], preferred_element_type=F32)
            .astype(BF16).reshape(count, COLS, size)
        )

    def late_block(c):
        at = pl.ds(pl.multiple_of((c - early) * COLS, 16), COLS)
        acc[:, at, others] = block(block_at(c), COLS, others)

    def piece(c, r):
        @pl.when(r == 0)
        def _():
            for n in range(steps):
                final_copy(c * steps + n).wait_recv()
            for k in range(slots):
                turned[k, :, block_at(c)] = vectors[k, block_at(c), :].T

        for n in range(2 * pairs):
            @pl.when(r == 1 + n)
            def _(n=n):
                half_of(c, n // 2, (n % 2) * (slots // 2))

        at = 2 * pairs

        for e in (early - 1, early):
            d = (e - early + 1) * 2

            @pl.when((c == e) & (r == at + 1))
            def _(d=d):
                early_block(d)

            @pl.when((c == e) & (r == at + 2))
            def _(d=d):
                early_block(d + 1)

            @pl.when((c == e) & (r == at + 3))
            def _(d=d, e=e):
                if e == early:
                    late_block(e)
                early_send(d)
                early_send(d + 1)

        @pl.when((c > early) & (r == at + 1))
        def _():
            early_block(c)

        @pl.when((c > early) & (r == at + 2))
        def _():
            late_block(c)

        @pl.when((c > early) & (r == at + 3))
        def _():
            early_send(c)

    def step(t, carry):
        @pl.when((t < items) & (t % slots == 0))
        def _():
            near_copy(t // slots).wait_recv()

        i = t - lag_r

        @pl.when((i >= 0) & (i < items))
        def _():
            @pl.when(z > 0)
            def _():
                right_copy(i).wait_recv()

            @pl.when(z == 0)
            def _():
                right_out[i] = local(i)
                right_copy(i).start()

            @pl.when((z > 0) & (z < last))
            def _():
                oz, unused = owner(i)
                right_out[i] = lax.select(oz == z, local(i), right_in[i])
                right_copy(i).start()

        j = t - lag_l

        @pl.when((j >= 0) & (j < items))
        def _():
            @pl.when(z < last)
            def _():
                left_copy(j).wait_recv()

            @pl.when(z == last)
            def _():
                left_out[j] = local(j)
                left_copy(j).start()

            @pl.when((z > 0) & (z < last))
            def _():
                oz, unused = owner(j)
                left_out[j] = lax.select(oz == z, local(j), left_in[j])
                left_copy(j).start()

        f = t - lag_f

        @pl.when((f >= 0) & (f < items))
        def _():
            oz, unused = owner(f)
            k, rows = f % slots, my_rows(f)

            @pl.when(z == 0)
            def _():
                vectors[k, rows, :] = lax.select(oz == z, local(f), left_in[f])

            @pl.when(z == last)
            def _():
                vectors[k, rows, :] = lax.select(oz == z, local(f), right_in[f])

            @pl.when((z > 0) & (z < last))
            def _():
                came = lax.select(oz < z, right_in[f], left_in[f])
                vectors[k, rows, :] = lax.select(oz == z, local(f), came)

            final_copy(f).start()

        @pl.when(t == first)
        def _():
            load.wait()

        @pl.when(t >= first)
        def _():
            piece((t - first) // steps, (t - first) % steps)

        return carry

    lax.fori_loop(0, first + chunks * steps, step, 0)

    def sub(cc):
        return pl.ds(pl.multiple_of(cc * tile, 16), tile)

    rest_out[:, :, mine] = block(tile_at(y, 1 - core), tile, mine).astype(BF16)
    rest_out[:, :, others] = acc[:, sub(1 - core), others].astype(BF16)
    rest_copy.start()
    acc[:, sub(core), mine] = block(tile_at(y, core), tile, mine)
    rest_copy.wait_recv()
    for d in range(chunks):
        cols = block_at((d + early) % chunks)
        y_copy(d).wait_recv()
        out_ref[:, :, cols] = (
            acc[:, sub(core), cols] + rest_in[:, :, cols].astype(F32) + y_in[d].astype(F32)
        )

    for c in range(chunks * SPLIT):
        near_copy(c).wait_send()
    for c in range(chunks):
        core_copy(c).wait_send()
        y_copy(c).wait_send()
    rest_copy.wait_send()

    def drain(i, carry):
        @pl.when(z < last)
        def _():
            right_copy(i).wait_send()

        @pl.when(z > 0)
        def _():
            left_copy(i).wait_send()

        final_copy(i).wait_send()
        return carry

    lax.fori_loop(0, items, drain, 0)


def on_device(pair_size, amplitudes, cholesky_vectors, owner_order):
    pairs, size, unused = amplitudes.shape
    slots = owner_order.shape[1]
    part = COLS // 2 // SPLIT
    chunks = size // COLS
    items = slots * chunks * SPLIT
    tile = size // 4
    dma = pltpu.SemaphoreType.DMA
    vmem = pltpu.VMEM
    return pl.pallas_call(
        functools.partial(kernel, pair_size // 2, slots),
        out_shape=jax.ShapeDtypeStruct((pairs, tile, size), F32),
        in_specs=[
            pl.BlockSpec(memory_space=pltpu.SMEM),
            pl.BlockSpec(memory_space=pl.ANY),
            pl.BlockSpec(memory_space=pltpu.VMEM),
        ],
        out_specs=pl.BlockSpec(memory_space=pltpu.VMEM),
        scratch_shapes=[
            vmem((pairs, size, size), BF16),
            vmem((chunks * SPLIT, part, size), BF16),
            vmem((items, part, size), BF16),
            vmem((items, part, size), BF16),
            vmem((items, part, size), BF16),
            vmem((items, part, size), BF16),
            vmem((slots, size, size), BF16),
            vmem((slots, size, size), BF16),
            vmem((pairs, slots, size, size), BF16),
            vmem((pairs, size // 2, size), F32),
            vmem((chunks, pairs, tile, COLS), BF16),
            vmem((chunks, pairs, tile, COLS), BF16),
            vmem((chunks, pairs, tile, COLS), F32),
            vmem((chunks, pairs, tile, COLS), BF16),
            vmem((chunks, pairs, tile, COLS), BF16),
            vmem((pairs, tile, size), BF16),
            vmem((pairs, tile, size), BF16),
            dma,
            dma((chunks * SPLIT,)), dma((chunks * SPLIT,)),
            dma((items,)), dma((items,)),
            dma((items,)), dma((items,)),
            dma((items,)), dma((items,)),
            dma((chunks,)), dma((chunks,)),
            dma((chunks,)), dma((chunks,)),
            dma, dma,
        ],
        compiler_params=pltpu.CompilerParams(
            collective_id=0, has_side_effects=True, vmem_limit_bytes=58 * 2 ** 20
        ),
        cost_estimate=pl.CostEstimate(
            flops=4 * pairs * slots * size ** 3, bytes_accessed=8 * pairs * size ** 2,
            transcendentals=0,
        ),
    )(owner_order, amplitudes, cholesky_vectors[0, 0])


def solution(mesh):
    placed = (P("pair", None, None), P("vgrp", "pair", None, None), P())
    return jax.shard_map(
        functools.partial(on_device, mesh.shape["pair"]), mesh=mesh, in_specs=placed,
        out_specs=P("pair", "vgrp", None), check_vma=False,
    )
```
